32 devices in a mesh: fsdp: 8 (over z, y), grp: 4 (over x, core).
Axes of the slice: x: 2, y: 2, z: 4, core: 2. Of those that a mesh axis runs over, the one named last changes fastest.
Arguments:
- weight: bfloat16 [26624, 8192], P('fsdp', 'grp'), may hold values from -6 to 6
Outputs:
- quantized: bfloat16 [26624, 8192], P('grp', 'fsdp')
- scales: float32 [208, 64], P('grp', 'fsdp')
The draws below stay inside these ranges and needn't reach their ends.
All inputs are finite; a program needn't handle non-finite values. Where the reference program divides by a largest or mean magnitude, that divisor is 1e-20 or more.
Results may differ from the reference program's by a relative error of at most 0.001.
Values sent between devices are 32-bit elements; how exact they have to be, the bound alone decides.
No kernel may reach another device: no remote copies, remote signals or barrier semaphores. Data moves between devices by JAX's collectives and lax.ppermute only.
A program may use at most 192 MiB of HBM per device.

```python
import math
import jax
import jax.numpy as jnp
import numpy as np
from jax import lax

D = 8192
HB = 512
BLOCK = 128
FF = 26624
N_FSDP = 8
N_GRP = 4


def steps_of(rng, extent, shards, low, top_value):
    def one(axis_at, blocks):
        draws = jax.random.uniform(jax.random.fold_in(jax.random.fold_in(rng, 6), axis_at), (blocks,), jnp.float32, low / len(shards), top_value / len(shards))
        return jnp.repeat(jnp.exp(draws), extent[axis_at] // blocks).reshape((-1,) + (1,) * (len(extent) - axis_at - 1))

    factor_of = one(*shards[0])
    for cut in shards[1:]:
        factor_of = factor_of * one(*cut)
    return factor_of


def noise(rng, extent, scale, bound, split=(), kind=jnp.bfloat16):
    values = scale * jax.random.normal(rng, extent, jnp.float32)
    if split:
        values = values * steps_of(rng, extent, split, -0.22, 0.18)
    return jnp.clip(values, -bound, bound).astype(kind)


def setup_inputs(seed: int = 0) -> dict:
    key_list = jax.random.split(jax.random.key(seed), 2)
    return {
        "weight": noise(key_list[0], (FF, D), 1.0, 6.0, ((0, 8), (1, 4))),
    }


def paley_signs():
    squares_set = set()
    for coord_one in range(5):
        for coord_two in range(5):
            if coord_one or coord_two:
                squares_set.add(((coord_one * coord_one + 2 * coord_two * coord_two) % 5, 2 * coord_one * coord_two % 5))
    conference = np.zeros((26, 26), np.float32)
    conference[0, 1:] = 1.0
    conference[1:, 0] = 1.0
    for row_elem in range(25):
        for col_elem in range(25):
            diff_one = (row_elem % 5 - col_elem % 5) % 5
            diff_two = (row_elem // 5 - col_elem // 5) % 5
            if diff_one or diff_two:
                conference[1 + row_elem, 1 + col_elem] = 1.0 if (diff_one, diff_two) in squares_set else -1.0
    plus_block = np.array([[1.0, 1.0], [1.0, -1.0]], np.float32)
    minus_block = np.array([[1.0, -1.0], [-1.0, -1.0]], np.float32)
    return (np.kron(conference, plus_block) + np.kron(np.eye(26, dtype=np.float32), minus_block)).astype(np.float32)

def sylvester(order):
    indices = jnp.arange(order, dtype=jnp.int32)
    parity = jnp.zeros((order, order), jnp.int32)
    for bit_pos in range(max(order.bit_length() - 1, 0)):
        parity = parity + (indices[:, None] >> bit_pos & 1) * (indices[None, :] >> bit_pos & 1)
    return (1 - 2 * (parity % 2)).astype(jnp.float32)

def apply_axis(values, matrix, axis_pos):
    product = jnp.tensordot(matrix, values, axes=([1], [axis_pos]), precision=lax.Precision.HIGHEST)
    return jnp.moveaxis(product, 0, axis_pos)

def apply_sylvester(values, order, axis_pos):
    inner_order = min(order, 32)
    outer_order = order // inner_order
    dims_now = values.shape
    values = values.reshape(dims_now[:axis_pos] + (outer_order, inner_order) + dims_now[axis_pos + 1:])
    values = apply_axis(values, sylvester(outer_order), axis_pos)
    values = apply_axis(values, sylvester(inner_order), axis_pos + 1)
    return values.reshape(dims_now)

def reference(weight):
    values = weight.astype(jnp.float32).reshape(HB, 52, D)
    values = apply_axis(values, jnp.asarray(paley_signs(), jnp.float32), 1)
    values = apply_sylvester(values, HB, 0)
    values = values.reshape(HB, 52, N_GRP, D // N_GRP)
    values = apply_axis(values, sylvester(N_GRP), 2)
    values = apply_sylvester(values, D // N_GRP, 3)
    values = values.reshape(HB, 52, N_GRP, N_FSDP, D // (N_GRP * N_FSDP))
    values = values.transpose(0, 1, 3, 2, 4).reshape(FF, D)
    values = values * (1.0 / math.sqrt(FF * D))
    blocks = values.reshape(FF // BLOCK, BLOCK, D // BLOCK, BLOCK)
    scales = lax.optimization_barrier(jnp.max(jnp.abs(blocks), axis=(1, 3)))
    quantized = (blocks / (scales[:, None, :, None] + 1e-06)).astype(jnp.bfloat16).reshape(FF, D)
    return (quantized, scales)
```

```python
import functools
import math

import jax
import jax.numpy as jnp
import numpy as np
from jax import lax
from jax.experimental import pallas as pl
from jax.experimental.pallas import tpu as pltpu
from jax.sharding import PartitionSpec as P

D = 8192
BLOCK = 128
FF = 26624
PALEY = 52
LANES = 128
SPLIT = 2
CHAINED = True


def paley_signs():
    squares_set = set()
    for coord_one in range(5):
        for coord_two in range(5):
            if coord_one or coord_two:
                squares_set.add(
                    (
                        (coord_one * coord_one + 2 * coord_two * coord_two) % 5,
                        2 * coord_one * coord_two % 5,
                    )
                )
    conference = np.zeros((26, 26), np.float32)
    conference[0, 1:] = 1.0
    conference[1:, 0] = 1.0
    for row_elem in range(25):
        for col_elem in range(25):
            diff_one = (row_elem % 5 - col_elem % 5) % 5
            diff_two = (row_elem // 5 - col_elem // 5) % 5
            if diff_one or diff_two:
                conference[1 + row_elem, 1 + col_elem] = (
                    1.0 if (diff_one, diff_two) in squares_set else -1.0
                )
    plus_block = np.array([[1.0, 1.0], [1.0, -1.0]], np.float32)
    minus_block = np.array([[1.0, -1.0], [-1.0, -1.0]], np.float32)
    return (
        np.kron(conference, plus_block) + np.kron(np.eye(26, dtype=np.float32), minus_block)
    ).astype(np.float32)


def sylvester(order):
    table = np.ones((1, 1), np.float32)
    while table.shape[0] < order:
        table = np.kron(np.array([[1.0, 1.0], [1.0, -1.0]], np.float32), table)
    return table


def sign_table(order, dtype):
    if order <= 64:
        indices = lax.iota(jnp.int32, order)
        parity = jnp.zeros((order, order), jnp.int32)
        for bit_pos in range(max(order.bit_length() - 1, 0)):
            parity = parity + (indices[:, None] >> bit_pos & 1) * (indices[None, :] >> bit_pos & 1)
        return (1 - 2 * (parity & 1)).astype(dtype)
    outer_part = sign_table(order // 64, dtype)
    inner_part = sign_table(64, dtype)
    return (outer_part[:, None, :, None] * inner_part[None, :, None, :]).reshape(order, order)


def plain_body(weight):
    exact_prec = lax.Precision.HIGHEST
    rows_dev, cols_dev = weight.shape
    parts = lax.axis_size("fsdp")
    groups = lax.axis_size("grp")
    sub_rows = rows_dev // 52
    piece = cols_dev // parts
    piece_signs = sign_table(piece, jnp.bfloat16)
    parts_signs = sign_table(parts, jnp.float32)
    paley = jnp.asarray(paley_signs(), jnp.float32)
    sub_signs = sign_table(sub_rows, jnp.float32)
    group_signs = sign_table(groups, jnp.float32)
    inner_done = jnp.einsum(
        "rab,bj->raj",
        weight.reshape(rows_dev, parts, piece),
        piece_signs,
        preferred_element_type=jnp.float32,
    )
    rotated = jnp.einsum("ap,raj->prj", parts_signs, inner_done, precision=exact_prec)
    rotated = rotated.reshape(parts, sub_rows, 52, piece)
    rotated = jnp.einsum("ab,pcbj->pcaj", paley, rotated, precision=exact_prec)
    rotated = jnp.einsum("ce,peaj->pcaj", sub_signs, rotated, precision=exact_prec)
    rotated = rotated.reshape(parts, sub_rows, 52 * piece)
    fsdp_signs = sign_table(parts, jnp.float32)
    mixed = jnp.einsum(
        "fg,gnx->fnx",
        fsdp_signs,
        lax.all_to_all(rotated, "fsdp", split_axis=0, concat_axis=0, tiled=True),
        precision=exact_prec,
    )
    count = mixed.shape[1]
    stacked = mixed.reshape(1, parts, count, 52 * piece)
    moved = lax.all_to_all(stacked, "grp", split_axis=1, concat_axis=0, tiled=True)
    moved = moved.reshape(groups, parts // groups, count, 52, piece)
    result = jnp.einsum("qg,gmnaj->mnaqj", group_signs, moved, precision=exact_prec)
    cols_out = groups * piece
    final = result.reshape(-1, cols_out) * (1.0 / math.sqrt(FF * D))
    rows_out = final.shape[0]
    blocks = final.reshape(rows_out // BLOCK, BLOCK, cols_out // BLOCK, BLOCK)
    scales = jnp.max(jnp.abs(blocks), axis=(1, 3))
    quantized = (
        (blocks / (scales[:, None, :, None] + 1e-06))
        .astype(jnp.bfloat16)
        .reshape(rows_out, cols_out)
    )
    return (quantized, scales)


def parity_sign(bits, order):
    parity = bits
    shift = 1
    while shift < order.bit_length():
        parity = parity ^ (parity >> shift)
        shift *= 2
    return 1.0 - 2.0 * (parity & 1).astype(jnp.float32)


def butterfly(values):
    values = list(values)
    half = 1
    while half < len(values):
        for low in range(len(values)):
            if not low & half:
                one, two = values[low], values[low + half]
                values[low], values[low + half] = one + two, one - two
        half *= 2
    return values


def compiler_params(limit):
    return pltpu.CompilerParams(vmem_limit_bytes=limit)


TINY = pl.CostEstimate(flops=0, bytes_accessed=0, transcendentals=0)
ANYWHERE = pl.BlockSpec(memory_space=pl.ANY)


class Labels:
    def __init__(self, parts, groups):
        self.parts_bits = parts.bit_length() - 1
        self.groups_bits = groups.bit_length() - 1
        self.slab_bits = self.parts_bits - self.groups_bits

    def start(self):
        return [("p", i) for i in range(self.parts_bits)]

    def split(self, axis, bit):
        return ("p" if axis == "fsdp" else "g", bit)

    def made(self, axis, bit):
        if axis == "grp":
            return ("k", bit)
        return ("m", bit) if bit < self.slab_bits else ("g", bit - self.slab_bits)


def slot_of(labels, values):
    return sum(values[label] << at for at, label in enumerate(labels))


def values_of(labels, slot):
    return {label: slot >> at & 1 for at, label in enumerate(labels)}


class Stage:
    def __init__(self, kind, bits):
        self.kind, self.bits = kind, bits
        self.fan = 1 << len(bits)

    def send(self, arrays):
        if self.kind == "all":
            return [lax.all_to_all(arrays[0], self.bits[0][0], split_axis=0, concat_axis=0, tiled=True)]
        if self.kind == "sum":
            axis, bit = self.bits[0]
            pairs = [[i, i ^ 1 << bit] for i in range(lax.axis_size(axis)) if not i >> bit & 1]
            both = lax.psum_scatter(
                arrays[0], axis, scatter_dimension=0, axis_index_groups=pairs, tiled=False
            )
            return [arrays[0], both]
        received = [arrays[0]]
        axes = {axis for axis, _ in self.bits}
        sizes = {axis: lax.axis_size(axis) for axis in axes}
        for e in range(1, self.fan):
            masks = {axis: 0 for axis in axes}
            for at, (axis, bit) in enumerate(self.bits):
                masks[axis] |= (e >> at & 1) << bit
            used = [axis for axis in ("fsdp", "grp") if masks.get(axis)]
            assert len(used) == 1
            axis = used[0]
            pairs = [(i, i ^ masks[axis]) for i in range(sizes[axis])]
            received.append(lax.ppermute(arrays[e], axis, pairs))
        return received

    def place(self):
        if self.kind == "all":
            return None
        place = 0
        for at, (axis, bit) in enumerate(self.bits):
            place = place | ((lax.axis_index(axis) >> bit) & 1) << at
        return place

    def arrived(self, refs, *index):
        if self.kind == "sum":
            axis, bit = self.bits[0]
            return [refs[0].at[(lax.axis_index(axis) >> bit & 1,) + index], refs[1].at[index]]
        return self.views(refs, self.fan, *index)

    def values(self, found):
        return [found[0], found[1] - found[0]] if self.kind == "sum" else found

    def views(self, refs, fan, *index):
        if self.kind != "xor":
            return [refs[0].at[(e,) + index] for e in range(fan)]
        return [refs[e].at[index] for e in range(fan)]

    def shapes(self, slots, rows, piece):
        if self.kind != "xor":
            return [jax.ShapeDtypeStruct((self.fan, slots, rows, piece), jnp.float32)]
        return [jax.ShapeDtypeStruct((slots, rows, piece), jnp.float32)] * self.fan

    def blocks(self, slots, rows, piece, moving, arrived=False):
        where = (lambda step: (0, step, 0)) if moving else (lambda step: (0, 0, 0))
        if self.kind != "xor":
            whole = pl.BlockSpec((self.fan, slots, rows, piece), lambda step: (0,) + where(step))
            after = [pl.BlockSpec((slots, rows, piece), where)] if self.kind == "sum" and arrived else []
            return [whole] + after
        return [pl.BlockSpec((slots, rows, piece), where)] * self.fan


def combine(stage, made, values, absolute=False):
    place, toward = stage.place(), None
    for at, label in enumerate(made):
        if label[0] == "g" and not absolute:
            bit = ((lax.axis_index("grp") >> label[1]) & 1) << at
            toward = bit if toward is None else toward | bit
    if toward is not None:
        values = [values[0]] + [
            parity_sign(toward & e, stage.fan) * values[e] for e in range(1, stage.fan)
        ]
    sums = butterfly(values)
    if place is not None:
        toward = 0 if toward is None else toward
        sums = [parity_sign((w ^ toward) & place, stage.fan) * sums[w] for w in range(stage.fan)]
    return sums


def make_pieces(weight, first, count, parts, after, stage, labels):
    rows_dev, cols_dev = weight.shape
    piece = cols_dev // parts
    sub_rows = rows_dev // PALEY
    rows = count * PALEY
    order = sylvester(sub_rows)
    base = jnp.asarray(np.kron(order[:count, :count], paley_signs()), jnp.bfloat16)
    inner = jnp.asarray(sylvester(piece), jnp.bfloat16)
    far_signs = order[first, ::count]
    names = labels.start()
    cut = [labels.split(*bit) for bit in stage.bits]
    rest_names = [name for name in names if name not in cut]

    def halves(values):
        high = values.astype(jnp.bfloat16)
        return high, (values - high.astype(jnp.float32)).astype(jnp.bfloat16)

    def kernel(base_ref, inner_ref, *refs):
        w_refs, refs = refs[:SPLIT], refs[SPLIT:]
        outs, held, summed = refs[len(after):-2], refs[-2], refs[-1]
        step = pl.program_id(0)
        me = None if stage.kind == "all" else lax.axis_index("fsdp")

        def gather(at, carry):
            here = pl.multiple_of(at * 16, 16)
            total = None
            for far, sign in enumerate(far_signs):
                part, inside = divmod(far * rows, rows_dev // SPLIT)
                term = w_refs[part][pl.ds(here + inside, 16), :].astype(jnp.float32)
                total = term if total is None else total + term if sign > 0 else total - term
            summed[pl.ds(here, 16), :] = total
            return carry

        lax.fori_loop(0, rows // 16, gather, 0)
        high, low = halves(summed[...])
        turned = jnp.dot(base_ref[...], high, preferred_element_type=jnp.float32) + jnp.dot(
            base_ref[...], low, preferred_element_type=jnp.float32
        )
        high, low = halves(turned)
        turned = jnp.dot(high, inner_ref[...], preferred_element_type=jnp.float32) + jnp.dot(
            low, inner_ref[...], preferred_element_type=jnp.float32
        )
        held[step] = turned

        @pl.when(step == parts - 1)
        def _():
            before = [1.0 if me is None else parity_sign(a & me, parts) for a in range(parts)]

            def body(at, carry):
                here = pl.ds(pl.multiple_of(at * 8, 8), 8)
                values = [held[a, here, :] for a in range(parts)]
                if me is not None:
                    values = [values[0]] + [before[a] * values[a] for a in range(1, parts)]
                for j, value in enumerate(butterfly(values)):
                    digits = values_of(names, j)
                    targets = stage.views(outs, stage.fan, slot_of(rest_names, digits), here)
                    targets[slot_of(cut, digits)][...] = value
                return carry

            lax.fori_loop(0, rows // 8, body, 0)

    whole = lambda step: (0, 0)
    slots = 1 << len(rest_names)
    return pl.pallas_call(
        kernel,
        grid=(parts,),
        in_specs=[
            pl.BlockSpec((rows, rows), whole, pipeline_mode=pl.Buffered(1)),
            pl.BlockSpec((piece, piece), whole, pipeline_mode=pl.Buffered(1)),
        ]
        + [
            pl.BlockSpec((rows_dev // SPLIT, piece), functools.partial(lambda part, step: (part, step), part))
            for part in range(SPLIT)
        ]
        + [ANYWHERE] * len(after),
        out_specs=stage.blocks(slots, rows, piece, False),
        out_shape=stage.shapes(slots, rows, piece),
        scratch_shapes=[
            pltpu.VMEM((parts, rows, piece), jnp.float32),
            pltpu.VMEM((rows, piece), jnp.float32),
        ],
        compiler_params=compiler_params(48 * 2**20),
        cost_estimate=TINY,
        name="make_pieces",
    )(base, inner, *[weight] * SPLIT, *after), rest_names


def mix_pieces(arrays, names, came, going, labels, after, absolute):
    rows, piece = arrays[0].shape[-2:]
    made = [labels.made(*bit) for bit in came.bits]
    cut = [labels.split(*bit) for bit in going.bits]
    rest_names = [name for name in names + made if name not in cut]
    slots_in, slots_out = 1 << len(names), 1 << len(rest_names)
    strip, tile = 8, rows
    for size in (104, 208):
        if rows % size == 0:
            tile = size

    def kernel(*refs):
        ins, outs = refs[: len(arrays)], refs[len(arrays) + len(after):]

        def body(at, carry):
            here = pl.ds(pl.multiple_of(at * strip, strip), strip)
            for slot in range(slots_in):
                values = came.values([view[...] for view in came.arrived(ins, slot, here)])
                for w, value in enumerate(combine(came, made, values, absolute)):
                    digits = {**values_of(names, slot), **values_of(made, w)}
                    target = going.views(outs, going.fan, slot_of(rest_names, digits), here)
                    if going.kind == "sum":
                        index = slot_of(cut, digits) ^ going.place()
                        outs[0][index, slot_of(rest_names, digits), here, :] = value
                    else:
                        target[slot_of(cut, digits)][...] = value
            return carry

        lax.fori_loop(0, tile // strip, body, 0)

    return pl.pallas_call(
        kernel,
        grid=(rows // tile,),
        in_specs=came.blocks(slots_in, tile, piece, True, True) + [ANYWHERE] * len(after),
        out_specs=going.blocks(slots_out, tile, piece, True),
        out_shape=going.shapes(slots_out, rows, piece),
        compiler_params=compiler_params(24 * 2**20),
        cost_estimate=TINY,
        name="mix_pieces",
    )(*arrays, *after), rest_names


def finish(target, chunks, low, high, rows_slab, groups, labels, after):
    piece = chunks[0][2][0].shape[-1]
    each = 1 << labels.slab_bits
    cols_out = groups * piece
    cols_blocks = cols_out // BLOCK
    blocks = [(m, b) for m in range(each) for b in range(low, high)]
    needed = [c for c in chunks if c[0] < high * BLOCK and c[1] > low * BLOCK]
    for c in needed:
        assert c[3] == needed[0][3] and c[4].bits == needed[0][4].bits
        assert c[4].kind == needed[0][4].kind
    names, came = needed[0][3], needed[0][4]
    made = [labels.made(*bit) for bit in came.bits]
    factor = 1.0 / math.sqrt(FF * D)
    operands = [array for c in needed for array in c[2]]
    starts = np.cumsum([0] + [len(c[2]) for c in needed])
    aliased = target is not None
    per_block = {
        b: [
            (at, max(c[0], b * BLOCK), min(c[1], (b + 1) * BLOCK))
            for at, c in enumerate(needed)
            if max(c[0], b * BLOCK) < min(c[1], (b + 1) * BLOCK)
        ]
        for b in range(low, high)
    }
    most = max(len(s) for s in per_block.values())
    slab_names = [name for name in names if name[0] == "m"]
    column_names = [name for name in names if name[0] == "k"]
    column_slots = 1 << len(column_names)

    def kernel(*refs):
        ins = refs[: len(operands)]
        out, scales_ref, held, ready, in_sems, out_sems = refs[
            len(operands) + int(aliased) + len(after):
        ]
        reads = []
        for at, (m, b) in enumerate(blocks):
            copies = []
            for seg, (c, start, stop) in enumerate(per_block[b]):
                base, sources = needed[c][0], ins[starts[c] : starts[c + 1]]
                for column in range(column_slots):
                    digits = {**values_of(slab_names, m), **values_of(column_names, column)}
                    views = came.arrived(
                        sources, slot_of(names, digits), pl.ds(start - base, stop - start)
                    )
                    for e, view in enumerate(views):
                        copy = pltpu.make_async_copy(
                            view,
                            held.at[at, column, e, pl.ds(start - b * BLOCK, stop - start), :],
                            in_sems.at[at, column, e, seg],
                        )
                        copy.start()
                        copies.append(copy)
            reads.append(copies)
        lane = lax.broadcasted_iota(jnp.int32, (1, cols_blocks), 1)
        writes = []
        for at, (m, b) in enumerate(blocks):
            for copy in reads[at]:
                copy.wait()
            found = jnp.zeros((1, cols_blocks), jnp.float32)
            for part in range(piece // BLOCK):
                span = pl.ds(part * BLOCK, BLOCK)
                for column in range(column_slots):
                    values = came.values([held[at, column, e, :, span] for e in range(came.fan)])
                    values = [value * factor for value in values]
                    for w, value in enumerate(combine(came, made, values)):
                        digits = {**values_of(column_names, column), **values_of(made, w)}
                        group = sum(bit << name[1] for name, bit in digits.items())
                        top = jnp.max(
                            jnp.max(jnp.abs(value), axis=0, keepdims=True), axis=1, keepdims=True
                        )
                        place = group * (piece // BLOCK) + part
                        found = jnp.where(lane == place, top, found)
                        ready[at, :, pl.ds(place * BLOCK, BLOCK)] = (
                            value * (1.0 / (top + 1e-06))
                        ).astype(jnp.bfloat16)
            scales_ref[pl.ds(at, 1), :] = found
            copy = pltpu.make_async_copy(
                ready.at[at],
                out.at[pl.ds(m * rows_slab + b * BLOCK, BLOCK), :],
                out_sems.at[at],
            )
            copy.start()
            writes.append(copy)
        for copy in writes:
            copy.wait()

    total = len(blocks)
    result, scales = pl.pallas_call(
        kernel,
        in_specs=[ANYWHERE] * (len(operands) + int(aliased) + len(after)),
        out_specs=[ANYWHERE, pl.BlockSpec(memory_space=pltpu.VMEM)],
        out_shape=[
            jax.ShapeDtypeStruct((each * rows_slab, cols_out), jnp.bfloat16),
            jax.ShapeDtypeStruct((total, cols_blocks), jnp.float32),
        ],
        scratch_shapes=[
            pltpu.VMEM((total, column_slots, came.fan, BLOCK, piece), jnp.float32),
            pltpu.VMEM((total, BLOCK, cols_out), jnp.bfloat16),
            pltpu.SemaphoreType.DMA((total, column_slots, came.fan, most)),
            pltpu.SemaphoreType.DMA((total,)),
        ],
        input_output_aliases={len(operands): 0} if aliased else {},
        compiler_params=compiler_params(28 * 2**20),
        cost_estimate=TINY,
        name="finish",
    )(*operands, *([target] if aliased else []), *after)
    return result, scales.reshape(each, high - low, cols_blocks)


def plan(sub_rows, labels):
    every = [("fsdp", i) for i in range(labels.parts_bits)]
    grp = [("grp", i) for i in range(labels.groups_bits)]
    eighth = sub_rows // 8
    sizes = [eighth // 2] * 2 + [eighth] * 7
    chunks = [(size, [Stage("all", every), Stage("xor", grp)]) for size in sizes]
    order = [0, 1]
    for c in range(len(chunks)):
        order += [c, c]
        if c + 2 < len(chunks):
            order += [c + 2]
    return chunks, order


def chunked_body(weight):
    rows_dev, cols_dev = weight.shape
    parts = lax.axis_size("fsdp")
    groups = lax.axis_size("grp")
    sub_rows = rows_dev // PALEY
    labels = Labels(parts, groups)
    chunks, order = plan(sub_rows, labels)
    chained = CHAINED
    firsts = np.cumsum([0] + [count for count, _ in chunks])
    state = {}
    result, scales, finished, token = None, [], [], ()
    for c in order:
        count, stages = chunks[c]
        if c not in state:
            arrays, names = make_pieces(
                weight, int(firsts[c]), count, parts, token, stages[0], labels
            )
            token = (arrays[0],) if chained else ()
            state[c] = (0, stages[0].send(arrays), names)
            continue
        at, arrays, names = state[c]
        absolute = any(s.kind == "all" and s.bits[0][0] == "grp" for s in stages)
        if at + 1 < len(stages):
            arrays, names = mix_pieces(arrays, names, stages[at], stages[at + 1], labels, token, absolute)
            token = (arrays[0],) if chained else ()
            state[c] = (at + 1, stages[at + 1].send(arrays), names)
            continue
        low, high = int(firsts[c]) * PALEY, int(firsts[c + 1]) * PALEY
        finished.append((low, high, arrays, names, stages[at]))
        ready = [
            b
            for b in range(low // BLOCK, -(-high // BLOCK))
            if sum(
                max(0, min(f[1], (b + 1) * BLOCK) - max(f[0], b * BLOCK)) for f in finished
            ) == BLOCK
        ]
        if ready:
            result, found = finish(
                result, finished, ready[0], ready[-1] + 1, rows_dev, groups, labels, token
            )
            token = (found,) if chained else ()
            scales.append((ready[0], found))
    scales = jnp.concatenate([found for _, found in sorted(scales, key=lambda s: s[0])], axis=1)
    return result, scales.reshape(-1, scales.shape[-1])


def body(weight):
    rows_dev, cols_dev = weight.shape
    parts = lax.axis_size("fsdp")
    groups = lax.axis_size("grp")
    tiled = (
        cols_dev % (parts * LANES) == 0
        and rows_dev % (8 * PALEY) == 0
        and rows_dev % BLOCK == 0
        and parts % groups == 0
        and parts <= 8
    )
    return chunked_body(weight) if tiled else plain_body(weight)


def solution(mesh):
    in_specs = (P("fsdp", "grp"),)
    out_specs = (P("grp", "fsdp"), P("grp", "fsdp"))
    return jax.shard_map(body, mesh=mesh, in_specs=in_specs, out_specs=out_specs, check_vma=False)
```

```python
import functools
import math

import jax
import jax.numpy as jnp
import numpy as np
from jax import lax
from jax.experimental import pallas as pl
from jax.experimental.pallas import tpu as pltpu
from jax.sharding import PartitionSpec as P

D = 8192
BLOCK = 128
FF = 26624
PALEY = 52
LANES = 128
SPLIT = 2


def paley_signs():
    squares_set = set()
    for coord_one in range(5):
        for coord_two in range(5):
            if coord_one or coord_two:
                squares_set.add(
                    (
                        (coord_one * coord_one + 2 * coord_two * coord_two) % 5,
                        2 * coord_one * coord_two % 5,
                    )
                )
    conference = np.zeros((26, 26), np.float32)
    conference[0, 1:] = 1.0
    conference[1:, 0] = 1.0
    for row_elem in range(25):
        for col_elem in range(25):
            diff_one = (row_elem % 5 - col_elem % 5) % 5
            diff_two = (row_elem // 5 - col_elem // 5) % 5
            if diff_one or diff_two:
                conference[1 + row_elem, 1 + col_elem] = (
                    1.0 if (diff_one, diff_two) in squares_set else -1.0
                )
    plus_block = np.array([[1.0, 1.0], [1.0, -1.0]], np.float32)
    minus_block = np.array([[1.0, -1.0], [-1.0, -1.0]], np.float32)
    return (
        np.kron(conference, plus_block) + np.kron(np.eye(26, dtype=np.float32), minus_block)
    ).astype(np.float32)


def sylvester(order):
    table = np.ones((1, 1), np.float32)
    while table.shape[0] < order:
        table = np.kron(np.array([[1.0, 1.0], [1.0, -1.0]], np.float32), table)
    return table


def sign_table(order, dtype):
    if order <= 64:
        indices = lax.iota(jnp.int32, order)
        parity = jnp.zeros((order, order), jnp.int32)
        for bit_pos in range(max(order.bit_length() - 1, 0)):
            parity = parity + (indices[:, None] >> bit_pos & 1) * (indices[None, :] >> bit_pos & 1)
        return (1 - 2 * (parity & 1)).astype(dtype)
    outer_part = sign_table(order // 64, dtype)
    inner_part = sign_table(64, dtype)
    return (outer_part[:, None, :, None] * inner_part[None, :, None, :]).reshape(order, order)


def plain_body(weight):
    exact_prec = lax.Precision.HIGHEST
    rows_dev, cols_dev = weight.shape
    parts = lax.axis_size("fsdp")
    groups = lax.axis_size("grp")
    sub_rows = rows_dev // 52
    piece = cols_dev // parts
    piece_signs = sign_table(piece, jnp.bfloat16)
    parts_signs = sign_table(parts, jnp.float32)
    paley = jnp.asarray(paley_signs(), jnp.float32)
    sub_signs = sign_table(sub_rows, jnp.float32)
    group_signs = sign_table(groups, jnp.float32)
    inner_done = jnp.einsum(
        "rab,bj->raj",
        weight.reshape(rows_dev, parts, piece),
        piece_signs,
        preferred_element_type=jnp.float32,
    )
    rotated = jnp.einsum("ap,raj->prj", parts_signs, inner_done, precision=exact_prec)
    rotated = rotated.reshape(parts, sub_rows, 52, piece)
    rotated = jnp.einsum("ab,pcbj->pcaj", paley, rotated, precision=exact_prec)
    rotated = jnp.einsum("ce,peaj->pcaj", sub_signs, rotated, precision=exact_prec)
    rotated = rotated.reshape(parts, sub_rows, 52 * piece)
    fsdp_signs = sign_table(parts, jnp.float32)
    mixed = jnp.einsum(
        "fg,gnx->fnx",
        fsdp_signs,
        lax.all_to_all(rotated, "fsdp", split_axis=0, concat_axis=0, tiled=True),
        precision=exact_prec,
    )
    count = mixed.shape[1]
    stacked = mixed.reshape(1, parts, count, 52 * piece)
    moved = lax.all_to_all(stacked, "grp", split_axis=1, concat_axis=0, tiled=True)
    moved = moved.reshape(groups, parts // groups, count, 52, piece)
    result = jnp.einsum("qg,gmnaj->mnaqj", group_signs, moved, precision=exact_prec)
    cols_out = groups * piece
    final = result.reshape(-1, cols_out) * (1.0 / math.sqrt(FF * D))
    rows_out = final.shape[0]
    blocks = final.reshape(rows_out // BLOCK, BLOCK, cols_out // BLOCK, BLOCK)
    scales = jnp.max(jnp.abs(blocks), axis=(1, 3))
    quantized = (
        (blocks / (scales[:, None, :, None] + 1e-06))
        .astype(jnp.bfloat16)
        .reshape(rows_out, cols_out)
    )
    return (quantized, scales)


def parity_sign(bits, order):
    parity = bits
    shift = 1
    while shift < order.bit_length():
        parity = parity ^ (parity >> shift)
        shift *= 2
    return 1.0 - 2.0 * (parity & 1).astype(jnp.float32)


def butterfly(values):
    values = list(values)
    half = 1
    while half < len(values):
        for low in range(len(values)):
            if not low & half:
                one, two = values[low], values[low + half]
                values[low], values[low + half] = one + two, one - two
        half *= 2
    return values


def compiler_params(limit):
    return pltpu.CompilerParams(vmem_limit_bytes=limit)


TINY = pl.CostEstimate(flops=0, bytes_accessed=0, transcendentals=0)
LONG = pl.CostEstimate(flops=10**12, bytes_accessed=4 * 10**9, transcendentals=0)
ANYWHERE = pl.BlockSpec(memory_space=pl.ANY)


class Labels:
    def __init__(self, parts, groups):
        self.parts_bits = parts.bit_length() - 1
        self.groups_bits = groups.bit_length() - 1
        self.slab_bits = self.parts_bits - self.groups_bits

    def start(self):
        return [("p", i) for i in range(self.parts_bits)]

    def split(self, axis, bit):
        return ("p" if axis == "fsdp" else "g", bit)

    def made(self, axis, bit):
        if axis == "grp":
            return ("k", bit)
        return ("m", bit) if bit < self.slab_bits else ("g", bit - self.slab_bits)


def slot_of(labels, values):
    return sum(values[label] << at for at, label in enumerate(labels))


def values_of(labels, slot):
    return {label: slot >> at & 1 for at, label in enumerate(labels)}


class Stage:
    def __init__(self, kind, bits):
        self.kind, self.bits = kind, bits
        self.fan = 1 << len(bits)

    def send(self, arrays):
        if self.kind == "all":
            return [lax.all_to_all(arrays[0], self.bits[0][0], split_axis=0, concat_axis=0, tiled=True)]
        if self.kind == "sum":
            axis, bit = self.bits[0]
            pairs = [[i, i ^ 1 << bit] for i in range(lax.axis_size(axis)) if not i >> bit & 1]
            both = lax.psum_scatter(
                arrays[0], axis, scatter_dimension=0, axis_index_groups=pairs, tiled=False
            )
            return [arrays[0], both]
        received = [arrays[0]]
        axes = {axis for axis, _ in self.bits}
        sizes = {axis: lax.axis_size(axis) for axis in axes}
        for e in range(1, self.fan):
            masks = {axis: 0 for axis in axes}
            for at, (axis, bit) in enumerate(self.bits):
                masks[axis] |= (e >> at & 1) << bit
            used = [axis for axis in ("fsdp", "grp") if masks.get(axis)]
            assert len(used) == 1
            axis = used[0]
            pairs = [(i, i ^ masks[axis]) for i in range(sizes[axis])]
            received.append(lax.ppermute(arrays[e], axis, pairs))
        return received

    def place(self):
        if self.kind == "all":
            return None
        place = 0
        for at, (axis, bit) in enumerate(self.bits):
            place = place | ((lax.axis_index(axis) >> bit) & 1) << at
        return place

    def arrived(self, refs, *index):
        if self.kind == "sum":
            axis, bit = self.bits[0]
            return [refs[0].at[(lax.axis_index(axis) >> bit & 1,) + index], refs[1].at[index]]
        return self.views(refs, self.fan, *index)

    def values(self, found):
        return [found[0], found[1] - found[0]] if self.kind == "sum" else found

    def views(self, refs, fan, *index):
        if self.kind != "xor":
            return [refs[0].at[(e,) + index] for e in range(fan)]
        return [refs[e].at[index] for e in range(fan)]

    def shapes(self, slots, rows, piece):
        if self.kind != "xor":
            return [jax.ShapeDtypeStruct((self.fan, slots, rows, piece), jnp.float32)]
        return [jax.ShapeDtypeStruct((slots, rows, piece), jnp.float32)] * self.fan

    def blocks(self, slots, rows, piece, moving, arrived=False):
        where = (lambda step: (0, step, 0)) if moving else (lambda step: (0, 0, 0))
        if self.kind != "xor":
            whole = pl.BlockSpec((self.fan, slots, rows, piece), lambda step: (0,) + where(step))
            after = [pl.BlockSpec((slots, rows, piece), where)] if self.kind == "sum" and arrived else []
            return [whole] + after
        return [pl.BlockSpec((slots, rows, piece), where)] * self.fan


def combine(stage, made, values, absolute=False):
    place, toward = stage.place(), None
    for at, label in enumerate(made):
        if label[0] == "g" and not absolute:
            bit = ((lax.axis_index("grp") >> label[1]) & 1) << at
            toward = bit if toward is None else toward | bit
    if toward is not None:
        values = [values[0]] + [
            parity_sign(toward & e, stage.fan) * values[e] for e in range(1, stage.fan)
        ]
    sums = butterfly(values)
    if place is not None:
        toward = 0 if toward is None else toward
        sums = [parity_sign((w ^ toward) & place, stage.fan) * sums[w] for w in range(stage.fan)]
    return sums


def make_pieces(weight, first, count, parts, after, stage, labels):
    rows_dev, cols_dev = weight.shape
    piece = cols_dev // parts
    sub_rows = rows_dev // PALEY
    rows = count * PALEY
    order = sylvester(sub_rows)
    base = jnp.asarray(np.kron(order[:count, :count], paley_signs()), jnp.bfloat16)
    inner = jnp.asarray(sylvester(piece), jnp.bfloat16)
    far_signs = order[first, ::count]
    names = labels.start()
    cut = [labels.split(*bit) for bit in stage.bits]
    rest_names = [name for name in names if name not in cut]

    def halves(values):
        high = values.astype(jnp.bfloat16)
        return high, (values - high.astype(jnp.float32)).astype(jnp.bfloat16)

    def kernel(base_ref, inner_ref, *refs):
        w_refs, refs = refs[:SPLIT], refs[SPLIT:]
        outs, held, summed = refs[len(after):-2], refs[-2], refs[-1]
        step = pl.program_id(0)
        me = None if stage.kind == "all" else lax.axis_index("fsdp")

        def gather(at, carry):
            here = pl.multiple_of(at * 16, 16)
            total = None
            for far, sign in enumerate(far_signs):
                part, inside = divmod(far * rows, rows_dev // SPLIT)
                term = w_refs[part][pl.ds(here + inside, 16), :].astype(jnp.float32)
                total = term if total is None else total + term if sign > 0 else total - term
            summed[pl.ds(here, 16), :] = total
            return carry

        lax.fori_loop(0, rows // 16, gather, 0)
        high, low = halves(summed[...])
        turned = jnp.dot(base_ref[...], high, preferred_element_type=jnp.float32) + jnp.dot(
            base_ref[...], low, preferred_element_type=jnp.float32
        )
        high, low = halves(turned)
        turned = jnp.dot(high, inner_ref[...], preferred_element_type=jnp.float32) + jnp.dot(
            low, inner_ref[...], preferred_element_type=jnp.float32
        )
        held[step] = turned

        @pl.when(step == parts - 1)
        def _():
            before = [1.0 if me is None else parity_sign(a & me, parts) for a in range(parts)]

            def body(at, carry):
                here = pl.ds(pl.multiple_of(at * 8, 8), 8)
                values = [held[a, here, :] for a in range(parts)]
                if me is not None:
                    values = [values[0]] + [before[a] * values[a] for a in range(1, parts)]
                for j, value in enumerate(butterfly(values)):
                    digits = values_of(names, j)
                    targets = stage.views(outs, stage.fan, slot_of(rest_names, digits), here)
                    targets[slot_of(cut, digits)][...] = value
                return carry

            lax.fori_loop(0, rows // 8, body, 0)

    whole = lambda step: (0, 0)
    slots = 1 << len(rest_names)
    return pl.pallas_call(
        kernel,
        grid=(parts,),
        in_specs=[
            pl.BlockSpec((rows, rows), whole, pipeline_mode=pl.Buffered(1)),
            pl.BlockSpec((piece, piece), whole, pipeline_mode=pl.Buffered(1)),
        ]
        + [
            pl.BlockSpec((rows_dev // SPLIT, piece), functools.partial(lambda part, step: (part, step), part))
            for part in range(SPLIT)
        ]
        + [ANYWHERE] * len(after),
        out_specs=stage.blocks(slots, rows, piece, False),
        out_shape=stage.shapes(slots, rows, piece),
        scratch_shapes=[
            pltpu.VMEM((parts, rows, piece), jnp.float32),
            pltpu.VMEM((rows, piece), jnp.float32),
        ],
        compiler_params=compiler_params(48 * 2**20),
        cost_estimate=TINY,
        name="make_pieces",
    )(base, inner, *[weight] * SPLIT, *after), rest_names


def mix_pieces(arrays, names, came, going, labels, after, absolute):
    rows, piece = arrays[0].shape[-2:]
    made = [labels.made(*bit) for bit in came.bits]
    cut = [labels.split(*bit) for bit in going.bits]
    rest_names = [name for name in names + made if name not in cut]
    slots_in, slots_out = 1 << len(names), 1 << len(rest_names)
    strip, tile = 8, rows
    for size in (104, 208):
        if rows % size == 0:
            tile = size

    def kernel(*refs):
        ins, outs = refs[: len(arrays)], refs[len(arrays) + len(after):]

        def body(at, carry):
            here = pl.ds(pl.multiple_of(at * strip, strip), strip)
            for slot in range(slots_in):
                values = came.values([view[...] for view in came.arrived(ins, slot, here)])
                for w, value in enumerate(combine(came, made, values, absolute)):
                    digits = {**values_of(names, slot), **values_of(made, w)}
                    target = going.views(outs, going.fan, slot_of(rest_names, digits), here)
                    if going.kind == "sum":
                        index = slot_of(cut, digits) ^ going.place()
                        outs[0][index, slot_of(rest_names, digits), here, :] = value
                    else:
                        target[slot_of(cut, digits)][...] = value
            return carry

        lax.fori_loop(0, tile // strip, body, 0)

    return pl.pallas_call(
        kernel,
        grid=(rows // tile,),
        in_specs=came.blocks(slots_in, tile, piece, True, True) + [ANYWHERE] * len(after),
        out_specs=going.blocks(slots_out, tile, piece, True),
        out_shape=going.shapes(slots_out, rows, piece),
        compiler_params=compiler_params(24 * 2**20),
        cost_estimate=TINY,
        name="mix_pieces",
    )(*arrays, *after), rest_names


def finish(target, chunks, low, high, rows_slab, groups, labels, after):
    piece = chunks[0][2][0].shape[-1]
    each = 1 << labels.slab_bits
    cols_out = groups * piece
    cols_blocks = cols_out // BLOCK
    blocks = [(m, b) for m in range(each) for b in range(low, high)]
    needed = [c for c in chunks if c[0] < high * BLOCK and c[1] > low * BLOCK]
    for c in needed:
        assert c[3] == needed[0][3] and c[4].bits == needed[0][4].bits
        assert c[4].kind == needed[0][4].kind
    names, came = needed[0][3], needed[0][4]
    made = [labels.made(*bit) for bit in came.bits]
    factor = 1.0 / math.sqrt(FF * D)
    operands = [array for c in needed for array in c[2]]
    starts = np.cumsum([0] + [len(c[2]) for c in needed])
    aliased = target is not None
    per_block = {
        b: [
            (at, max(c[0], b * BLOCK), min(c[1], (b + 1) * BLOCK))
            for at, c in enumerate(needed)
            if max(c[0], b * BLOCK) < min(c[1], (b + 1) * BLOCK)
        ]
        for b in range(low, high)
    }
    most = max(len(s) for s in per_block.values())
    slab_names = [name for name in names if name[0] == "m"]
    column_names = [name for name in names if name[0] == "k"]
    column_slots = 1 << len(column_names)

    def kernel(*refs):
        ins = refs[: len(operands)]
        out, scales_ref, held, ready, in_sems, out_sems = refs[
            len(operands) + int(aliased) + len(after):
        ]
        reads = []
        for at, (m, b) in enumerate(blocks):
            copies = []
            for seg, (c, start, stop) in enumerate(per_block[b]):
                base, sources = needed[c][0], ins[starts[c] : starts[c + 1]]
                for column in range(column_slots):
                    digits = {**values_of(slab_names, m), **values_of(column_names, column)}
                    views = came.arrived(
                        sources, slot_of(names, digits), pl.ds(start - base, stop - start)
                    )
                    for e, view in enumerate(views):
                        copy = pltpu.make_async_copy(
                            view,
                            held.at[at, column, e, pl.ds(start - b * BLOCK, stop - start), :],
                            in_sems.at[at, column, e, seg],
                        )
                        copy.start()
                        copies.append(copy)
            reads.append(copies)
        lane = lax.broadcasted_iota(jnp.int32, (1, cols_blocks), 1)
        writes = []
        for at, (m, b) in enumerate(blocks):
            for copy in reads[at]:
                copy.wait()
            found = jnp.zeros((1, cols_blocks), jnp.float32)
            for part in range(piece // BLOCK):
                span = pl.ds(part * BLOCK, BLOCK)
                for column in range(column_slots):
                    values = came.values([held[at, column, e, :, span] for e in range(came.fan)])
                    values = [value * factor for value in values]
                    for w, value in enumerate(combine(came, made, values)):
                        digits = {**values_of(column_names, column), **values_of(made, w)}
                        group = sum(bit << name[1] for name, bit in digits.items())
                        top = jnp.max(
                            jnp.max(jnp.abs(value), axis=0, keepdims=True), axis=1, keepdims=True
                        )
                        place = group * (piece // BLOCK) + part
                        found = jnp.where(lane == place, top, found)
                        ready[at, :, pl.ds(place * BLOCK, BLOCK)] = (
                            value * (1.0 / (top + 1e-06))
                        ).astype(jnp.bfloat16)
            scales_ref[pl.ds(at, 1), :] = found
            copy = pltpu.make_async_copy(
                ready.at[at],
                out.at[pl.ds(m * rows_slab + b * BLOCK, BLOCK), :],
                out_sems.at[at],
            )
            copy.start()
            writes.append(copy)
        for copy in writes:
            copy.wait()

    total = len(blocks)
    result, scales = pl.pallas_call(
        kernel,
        in_specs=[ANYWHERE] * (len(operands) + int(aliased) + len(after)),
        out_specs=[ANYWHERE, pl.BlockSpec(memory_space=pltpu.VMEM)],
        out_shape=[
            jax.ShapeDtypeStruct((each * rows_slab, cols_out), jnp.bfloat16),
            jax.ShapeDtypeStruct((total, cols_blocks), jnp.float32),
        ],
        scratch_shapes=[
            pltpu.VMEM((total, column_slots, came.fan, BLOCK, piece), jnp.float32),
            pltpu.VMEM((total, BLOCK, cols_out), jnp.bfloat16),
            pltpu.SemaphoreType.DMA((total, column_slots, came.fan, most)),
            pltpu.SemaphoreType.DMA((total,)),
        ],
        input_output_aliases={len(operands): 0} if aliased else {},
        compiler_params=compiler_params(28 * 2**20),
        cost_estimate=LONG,
        name="finish",
    )(*operands, *([target] if aliased else []), *after)
    return result, scales.reshape(each, high - low, cols_blocks)


def plan(sub_rows, labels):
    every = [("fsdp", i) for i in range(labels.parts_bits)]
    grp = [("grp", i) for i in range(labels.groups_bits)]
    unit = sub_rows // 16
    stages = [Stage("all", every), Stage("xor", grp)]
    chunks = [(unit * times, stages) for times in (1, 1, 2, 4, 4, 2, 1, 1)]
    n = len(chunks)
    order = [0, 1]
    for c in range(n):
        if c >= 1 and c < n - 1:
            order += [c - 1]
        order += [c]
        if c + 2 < n:
            order += [c + 2]
    return chunks, order + [n - 2, n - 1]


def chunked_body(weight):
    rows_dev, cols_dev = weight.shape
    parts = lax.axis_size("fsdp")
    groups = lax.axis_size("grp")
    sub_rows = rows_dev // PALEY
    labels = Labels(parts, groups)
    chunks, order = plan(sub_rows, labels)
    firsts = np.cumsum([0] + [count for count, _ in chunks])
    state = {}
    result, scales, finished, token = None, [], [], ()
    for c in order:
        count, stages = chunks[c]
        if c not in state:
            arrays, names = make_pieces(
                weight, int(firsts[c]), count, parts, token, stages[0], labels
            )
            token = (arrays[0],)
            state[c] = (0, stages[0].send(arrays), names)
            continue
        at, arrays, names = state[c]
        absolute = any(s.kind == "all" and s.bits[0][0] == "grp" for s in stages)
        if at + 1 < len(stages):
            arrays, names = mix_pieces(arrays, names, stages[at], stages[at + 1], labels, token, absolute)
            token = (arrays[0],)
            state[c] = (at + 1, stages[at + 1].send(arrays), names)
            continue
        low, high = int(firsts[c]) * PALEY, int(firsts[c + 1]) * PALEY
        finished.append((low, high, arrays, names, stages[at]))
        ready = [
            b
            for b in range(low // BLOCK, -(-high // BLOCK))
            if sum(
                max(0, min(f[1], (b + 1) * BLOCK) - max(f[0], b * BLOCK)) for f in finished
            ) == BLOCK
        ]
        if ready:
            result, found = finish(
                result, finished, ready[0], ready[-1] + 1, rows_dev, groups, labels, token
            )
            token = (found,)
            scales.append((ready[0], found))
    scales = jnp.concatenate([found for _, found in sorted(scales, key=lambda s: s[0])], axis=1)
    return result, scales.reshape(-1, scales.shape[-1])


def body(weight):
    rows_dev, cols_dev = weight.shape
    parts = lax.axis_size("fsdp")
    groups = lax.axis_size("grp")
    tiled = (
        cols_dev % (parts * LANES) == 0
        and rows_dev % (8 * PALEY) == 0
        and rows_dev % BLOCK == 0
        and parts % groups == 0
        and parts <= 8
    )
    return chunked_body(weight) if tiled else plain_body(weight)


def solution(mesh):
    in_specs = (P("fsdp", "grp"),)
    out_specs = (P("grp", "fsdp"), P("grp", "fsdp"))
    return jax.shard_map(body, mesh=mesh, in_specs=in_specs, out_specs=out_specs, check_vma=False)
```

```python
import functools
import math

import jax
import jax.numpy as jnp
import numpy as np
from jax import lax
from jax.experimental import pallas as pl
from jax.experimental.pallas import tpu as pltpu
from jax.sharding import PartitionSpec as P

D = 8192
BLOCK = 128
FF = 26624
PALEY = 52
LANES = 128
SPLIT = 2


def paley_signs():
    squares_set = set()
    for coord_one in range(5):
        for coord_two in range(5):
            if coord_one or coord_two:
                squares_set.add(
                    (
                        (coord_one * coord_one + 2 * coord_two * coord_two) % 5,
                        2 * coord_one * coord_two % 5,
                    )
                )
    conference = np.zeros((26, 26), np.float32)
    conference[0, 1:] = 1.0
    conference[1:, 0] = 1.0
    for row_elem in range(25):
        for col_elem in range(25):
            diff_one = (row_elem % 5 - col_elem % 5) % 5
            diff_two = (row_elem // 5 - col_elem // 5) % 5
            if diff_one or diff_two:
                conference[1 + row_elem, 1 + col_elem] = (
                    1.0 if (diff_one, diff_two) in squares_set else -1.0
                )
    plus_block = np.array([[1.0, 1.0], [1.0, -1.0]], np.float32)
    minus_block = np.array([[1.0, -1.0], [-1.0, -1.0]], np.float32)
    return (
        np.kron(conference, plus_block) + np.kron(np.eye(26, dtype=np.float32), minus_block)
    ).astype(np.float32)


def sylvester(order):
    table = np.ones((1, 1), np.float32)
    while table.shape[0] < order:
        table = np.kron(np.array([[1.0, 1.0], [1.0, -1.0]], np.float32), table)
    return table


def sign_table(order, dtype):
    if order <= 64:
        indices = lax.iota(jnp.int32, order)
        parity = jnp.zeros((order, order), jnp.int32)
        for bit_pos in range(max(order.bit_length() - 1, 0)):
            parity = parity + (indices[:, None] >> bit_pos & 1) * (indices[None, :] >> bit_pos & 1)
        return (1 - 2 * (parity & 1)).astype(dtype)
    outer_part = sign_table(order // 64, dtype)
    inner_part = sign_table(64, dtype)
    return (outer_part[:, None, :, None] * inner_part[None, :, None, :]).reshape(order, order)


def plain_body(weight):
    exact_prec = lax.Precision.HIGHEST
    rows_dev, cols_dev = weight.shape
    parts = lax.axis_size("fsdp")
    groups = lax.axis_size("grp")
    sub_rows = rows_dev // 52
    piece = cols_dev // parts
    piece_signs = sign_table(piece, jnp.bfloat16)
    parts_signs = sign_table(parts, jnp.float32)
    paley = jnp.asarray(paley_signs(), jnp.float32)
    sub_signs = sign_table(sub_rows, jnp.float32)
    group_signs = sign_table(groups, jnp.float32)
    inner_done = jnp.einsum(
        "rab,bj->raj",
        weight.reshape(rows_dev, parts, piece),
        piece_signs,
        preferred_element_type=jnp.float32,
    )
    rotated = jnp.einsum("ap,raj->prj", parts_signs, inner_done, precision=exact_prec)
    rotated = rotated.reshape(parts, sub_rows, 52, piece)
    rotated = jnp.einsum("ab,pcbj->pcaj", paley, rotated, precision=exact_prec)
    rotated = jnp.einsum("ce,peaj->pcaj", sub_signs, rotated, precision=exact_prec)
    rotated = rotated.reshape(parts, sub_rows, 52 * piece)
    fsdp_signs = sign_table(parts, jnp.float32)
    mixed = jnp.einsum(
        "fg,gnx->fnx",
        fsdp_signs,
        lax.all_to_all(rotated, "fsdp", split_axis=0, concat_axis=0, tiled=True),
        precision=exact_prec,
    )
    count = mixed.shape[1]
    stacked = mixed.reshape(1, parts, count, 52 * piece)
    moved = lax.all_to_all(stacked, "grp", split_axis=1, concat_axis=0, tiled=True)
    moved = moved.reshape(groups, parts // groups, count, 52, piece)
    result = jnp.einsum("qg,gmnaj->mnaqj", group_signs, moved, precision=exact_prec)
    cols_out = groups * piece
    final = result.reshape(-1, cols_out) * (1.0 / math.sqrt(FF * D))
    rows_out = final.shape[0]
    blocks = final.reshape(rows_out // BLOCK, BLOCK, cols_out // BLOCK, BLOCK)
    scales = jnp.max(jnp.abs(blocks), axis=(1, 3))
    quantized = (
        (blocks / (scales[:, None, :, None] + 1e-06))
        .astype(jnp.bfloat16)
        .reshape(rows_out, cols_out)
    )
    return (quantized, scales)


def parity_sign(bits, order):
    parity = bits
    shift = 1
    while shift < order.bit_length():
        parity = parity ^ (parity >> shift)
        shift *= 2
    return 1.0 - 2.0 * (parity & 1).astype(jnp.float32)


def butterfly(values):
    values = list(values)
    half = 1
    while half < len(values):
        for low in range(len(values)):
            if not low & half:
                one, two = values[low], values[low + half]
                values[low], values[low + half] = one + two, one - two
        half *= 2
    return values


def compiler_params(limit):
    return pltpu.CompilerParams(vmem_limit_bytes=limit)


TINY = pl.CostEstimate(flops=0, bytes_accessed=0, transcendentals=0)
LONG = pl.CostEstimate(flops=10**12, bytes_accessed=4 * 10**9, transcendentals=0)
ANYWHERE = pl.BlockSpec(memory_space=pl.ANY)


class Labels:
    def __init__(self, parts, groups):
        self.parts_bits = parts.bit_length() - 1
        self.groups_bits = groups.bit_length() - 1
        self.slab_bits = self.parts_bits - self.groups_bits

    def start(self):
        return [("p", i) for i in range(self.parts_bits)]

    def split(self, axis, bit):
        return ("p" if axis == "fsdp" else "g", bit)

    def made(self, axis, bit):
        if axis == "grp":
            return ("k", bit)
        return ("m", bit) if bit < self.slab_bits else ("g", bit - self.slab_bits)


def slot_of(labels, values):
    return sum(values[label] << at for at, label in enumerate(labels))


def values_of(labels, slot):
    return {label: slot >> at & 1 for at, label in enumerate(labels)}


class Stage:
    def __init__(self, kind, bits):
        self.kind, self.bits = kind, bits
        self.fan = 1 << len(bits)

    def send(self, arrays):
        if self.kind == "all":
            return [lax.all_to_all(arrays[0], self.bits[0][0], split_axis=0, concat_axis=0, tiled=True)]
        if self.kind == "sum":
            axis, bit = self.bits[0]
            pairs = [[i, i ^ 1 << bit] for i in range(lax.axis_size(axis)) if not i >> bit & 1]
            both = lax.psum_scatter(
                arrays[0], axis, scatter_dimension=0, axis_index_groups=pairs, tiled=False
            )
            return [arrays[0], both]
        received = [arrays[0]]
        axes = {axis for axis, _ in self.bits}
        sizes = {axis: lax.axis_size(axis) for axis in axes}
        for e in range(1, self.fan):
            masks = {axis: 0 for axis in axes}
            for at, (axis, bit) in enumerate(self.bits):
                masks[axis] |= (e >> at & 1) << bit
            used = [axis for axis in ("fsdp", "grp") if masks.get(axis)]
            assert len(used) == 1
            axis = used[0]
            pairs = [(i, i ^ masks[axis]) for i in range(sizes[axis])]
            received.append(lax.ppermute(arrays[e], axis, pairs))
        return received

    def place(self):
        if self.kind == "all":
            return None
        place = 0
        for at, (axis, bit) in enumerate(self.bits):
            place = place | ((lax.axis_index(axis) >> bit) & 1) << at
        return place

    def arrived(self, refs, *index):
        if self.kind == "sum":
            axis, bit = self.bits[0]
            return [refs[0].at[(lax.axis_index(axis) >> bit & 1,) + index], refs[1].at[index]]
        return self.views(refs, self.fan, *index)

    def values(self, found):
        return [found[0], found[1] - found[0]] if self.kind == "sum" else found

    def views(self, refs, fan, *index):
        if self.kind != "xor":
            return [refs[0].at[(e,) + index] for e in range(fan)]
        return [refs[e].at[index] for e in range(fan)]

    def shapes(self, slots, rows, piece):
        if self.kind != "xor":
            return [jax.ShapeDtypeStruct((self.fan, slots, rows, piece), jnp.float32)]
        return [jax.ShapeDtypeStruct((slots, rows, piece), jnp.float32)] * self.fan

    def blocks(self, slots, rows, piece, arrived=False):
        where = lambda at, *inner: (0, at, 0)
        if self.kind != "xor":
            whole = pl.BlockSpec((self.fan, slots, rows, piece), lambda *at: (0,) + where(*at))
            after = [pl.BlockSpec((slots, rows, piece), where)] if self.kind == "sum" and arrived else []
            return [whole] + after
        return [pl.BlockSpec((slots, rows, piece), where)] * self.fan


def combine(stage, made, values, absolute=False):
    place, toward = stage.place(), None
    for at, label in enumerate(made):
        if label[0] == "g" and not absolute:
            bit = ((lax.axis_index("grp") >> label[1]) & 1) << at
            toward = bit if toward is None else toward | bit
    if toward is not None:
        values = [values[0]] + [
            parity_sign(toward & e, stage.fan) * values[e] for e in range(1, stage.fan)
        ]
    sums = butterfly(values)
    if place is not None:
        toward = 0 if toward is None else toward
        sums = [parity_sign((w ^ toward) & place, stage.fan) * sums[w] for w in range(stage.fan)]
    return sums


def make_pieces(weight, first, count, at_once, parts, after, stage, labels):
    rows_dev, cols_dev = weight.shape
    piece = cols_dev // parts
    sub_rows = rows_dev // PALEY
    rows = at_once * PALEY
    base = jnp.asarray(np.kron(sylvester(at_once), paley_signs()), jnp.bfloat16)
    inner = jnp.asarray(sylvester(piece), jnp.bfloat16)
    names = labels.start()
    cut = [labels.split(*bit) for bit in stage.bits]
    rest_names = [name for name in names if name not in cut]

    def halves(values):
        high = values.astype(jnp.bfloat16)
        return high, (values - high.astype(jnp.float32)).astype(jnp.bfloat16)

    def kernel(base_ref, inner_ref, *refs):
        w_refs, refs = refs[:SPLIT], refs[SPLIT:]
        outs, held, summed = refs[len(after):-2], refs[-2], refs[-1]
        turn, step = pl.program_id(0), pl.program_id(1)
        far_signs = [
            parity_sign((first + turn * at_once) & far, sub_rows)
            for far in range(0, sub_rows, at_once)
        ]
        me = None if stage.kind == "all" else lax.axis_index("fsdp")

        def gather(at, carry):
            here = pl.multiple_of(at * 16, 16)
            total = None
            for far, sign in enumerate(far_signs):
                part, inside = divmod(far * rows, rows_dev // SPLIT)
                term = w_refs[part][pl.ds(here + inside, 16), :].astype(jnp.float32)
                total = term if total is None else total + sign * term
            summed[pl.ds(here, 16), :] = total
            return carry

        lax.fori_loop(0, rows // 16, gather, 0)
        high, low = halves(summed[...])
        turned = jnp.dot(base_ref[...], high, preferred_element_type=jnp.float32) + jnp.dot(
            base_ref[...], low, preferred_element_type=jnp.float32
        )
        high, low = halves(turned)
        turned = jnp.dot(high, inner_ref[...], preferred_element_type=jnp.float32) + jnp.dot(
            low, inner_ref[...], preferred_element_type=jnp.float32
        )
        held[step] = turned

        @pl.when(step == parts - 1)
        def _():
            before = [1.0 if me is None else parity_sign(a & me, parts) for a in range(parts)]

            def body(at, carry):
                here = pl.ds(pl.multiple_of(at * 8, 8), 8)
                values = [held[a, here, :] for a in range(parts)]
                if me is not None:
                    values = [values[0]] + [before[a] * values[a] for a in range(1, parts)]
                for j, value in enumerate(butterfly(values)):
                    digits = values_of(names, j)
                    targets = stage.views(outs, stage.fan, slot_of(rest_names, digits), here)
                    targets[slot_of(cut, digits)][...] = value
                return carry

            lax.fori_loop(0, rows // 8, body, 0)

    whole = lambda turn, step: (0, 0)
    slots = 1 << len(rest_names)
    return pl.pallas_call(
        kernel,
        grid=(count // at_once, parts),
        in_specs=[
            pl.BlockSpec((rows, rows), whole, pipeline_mode=pl.Buffered(1)),
            pl.BlockSpec((piece, piece), whole, pipeline_mode=pl.Buffered(1)),
        ]
        + [
            pl.BlockSpec((rows_dev // SPLIT, piece), functools.partial(lambda part, turn, step: (part, step), part))
            for part in range(SPLIT)
        ]
        + [ANYWHERE] * len(after),
        out_specs=stage.blocks(slots, rows, piece),
        out_shape=stage.shapes(slots, count * PALEY, piece),
        scratch_shapes=[
            pltpu.VMEM((parts, rows, piece), jnp.float32),
            pltpu.VMEM((rows, piece), jnp.float32),
        ],
        compiler_params=compiler_params(48 * 2**20),
        cost_estimate=TINY,
        name="make_pieces",
    )(base, inner, *[weight] * SPLIT, *after), rest_names


def mix_pieces(arrays, names, came, going, labels, after, absolute):
    rows, piece = arrays[0].shape[-2:]
    made = [labels.made(*bit) for bit in came.bits]
    cut = [labels.split(*bit) for bit in going.bits]
    rest_names = [name for name in names + made if name not in cut]
    slots_in, slots_out = 1 << len(names), 1 << len(rest_names)
    strip, tile = 8, rows
    for size in (104, 208):
        if rows % size == 0:
            tile = size

    def kernel(*refs):
        ins, outs = refs[: len(arrays)], refs[len(arrays) + len(after):]

        def body(at, carry):
            here = pl.ds(pl.multiple_of(at * strip, strip), strip)
            for slot in range(slots_in):
                values = came.values([view[...] for view in came.arrived(ins, slot, here)])
                for w, value in enumerate(combine(came, made, values, absolute)):
                    digits = {**values_of(names, slot), **values_of(made, w)}
                    target = going.views(outs, going.fan, slot_of(rest_names, digits), here)
                    if going.kind == "sum":
                        index = slot_of(cut, digits) ^ going.place()
                        outs[0][index, slot_of(rest_names, digits), here, :] = value
                    else:
                        target[slot_of(cut, digits)][...] = value
            return carry

        lax.fori_loop(0, tile // strip, body, 0)

    return pl.pallas_call(
        kernel,
        grid=(rows // tile,),
        in_specs=came.blocks(slots_in, tile, piece, True) + [ANYWHERE] * len(after),
        out_specs=going.blocks(slots_out, tile, piece),
        out_shape=going.shapes(slots_out, rows, piece),
        compiler_params=compiler_params(24 * 2**20),
        cost_estimate=TINY,
        name="mix_pieces",
    )(*arrays, *after), rest_names


def finish(target, chunks, low, high, rows_slab, groups, labels, after):
    piece = chunks[0][2][0].shape[-1]
    each = 1 << labels.slab_bits
    cols_out = groups * piece
    cols_blocks = cols_out // BLOCK
    blocks = [(m, b) for m in range(each) for b in range(low, high)]
    needed = [c for c in chunks if c[0] < high * BLOCK and c[1] > low * BLOCK]
    for c in needed:
        assert c[3] == needed[0][3] and c[4].bits == needed[0][4].bits
        assert c[4].kind == needed[0][4].kind
    names, came = needed[0][3], needed[0][4]
    made = [labels.made(*bit) for bit in came.bits]
    factor = 1.0 / math.sqrt(FF * D)
    operands = [array for c in needed for array in c[2]]
    starts = np.cumsum([0] + [len(c[2]) for c in needed])
    aliased = target is not None
    per_block = {
        b: [
            (at, max(c[0], b * BLOCK), min(c[1], (b + 1) * BLOCK))
            for at, c in enumerate(needed)
            if max(c[0], b * BLOCK) < min(c[1], (b + 1) * BLOCK)
        ]
        for b in range(low, high)
    }
    most = max(len(s) for s in per_block.values())
    slab_names = [name for name in names if name[0] == "m"]
    column_names = [name for name in names if name[0] == "k"]
    column_slots = 1 << len(column_names)

    def kernel(*refs):
        ins = refs[: len(operands)]
        out, scales_ref, held, ready, in_sems, out_sems = refs[
            len(operands) + int(aliased) + len(after):
        ]
        reads = []
        for at, (m, b) in enumerate(blocks):
            copies = []
            for seg, (c, start, stop) in enumerate(per_block[b]):
                base, sources = needed[c][0], ins[starts[c] : starts[c + 1]]
                for column in range(column_slots):
                    digits = {**values_of(slab_names, m), **values_of(column_names, column)}
                    views = came.arrived(
                        sources, slot_of(names, digits), pl.ds(start - base, stop - start)
                    )
                    for e, view in enumerate(views):
                        copy = pltpu.make_async_copy(
                            view,
                            held.at[at, column, e, pl.ds(start - b * BLOCK, stop - start), :],
                            in_sems.at[at, column, e, seg],
                        )
                        copy.start()
                        copies.append(copy)
            reads.append(copies)
        lane = lax.broadcasted_iota(jnp.int32, (1, cols_blocks), 1)
        writes = []
        for at, (m, b) in enumerate(blocks):
            for copy in reads[at]:
                copy.wait()
            found = jnp.zeros((1, cols_blocks), jnp.float32)
            for part in range(piece // BLOCK):
                span = pl.ds(part * BLOCK, BLOCK)
                for column in range(column_slots):
                    values = came.values([held[at, column, e, :, span] for e in range(came.fan)])
                    values = [value * factor for value in values]
                    for w, value in enumerate(combine(came, made, values)):
                        digits = {**values_of(column_names, column), **values_of(made, w)}
                        group = sum(bit << name[1] for name, bit in digits.items())
                        top = jnp.max(
                            jnp.max(jnp.abs(value), axis=0, keepdims=True), axis=1, keepdims=True
                        )
                        place = group * (piece // BLOCK) + part
                        found = jnp.where(lane == place, top, found)
                        ready[at, :, pl.ds(place * BLOCK, BLOCK)] = (
                            value * (1.0 / (top + 1e-06))
                        ).astype(jnp.bfloat16)
            scales_ref[pl.ds(at, 1), :] = found
            copy = pltpu.make_async_copy(
                ready.at[at],
                out.at[pl.ds(m * rows_slab + b * BLOCK, BLOCK), :],
                out_sems.at[at],
            )
            copy.start()
            writes.append(copy)
        for copy in writes:
            copy.wait()

    total = len(blocks)
    result, scales = pl.pallas_call(
        kernel,
        in_specs=[ANYWHERE] * (len(operands) + int(aliased) + len(after)),
        out_specs=[ANYWHERE, pl.BlockSpec(memory_space=pltpu.VMEM)],
        out_shape=[
            jax.ShapeDtypeStruct((each * rows_slab, cols_out), jnp.bfloat16),
            jax.ShapeDtypeStruct((total, cols_blocks), jnp.float32),
        ],
        scratch_shapes=[
            pltpu.VMEM((total, column_slots, came.fan, BLOCK, piece), jnp.float32),
            pltpu.VMEM((total, BLOCK, cols_out), jnp.bfloat16),
            pltpu.SemaphoreType.DMA((total, column_slots, came.fan, most)),
            pltpu.SemaphoreType.DMA((total,)),
        ],
        input_output_aliases={len(operands): 0} if aliased else {},
        compiler_params=compiler_params(28 * 2**20),
        cost_estimate=LONG,
        name="finish",
    )(*operands, *([target] if aliased else []), *after)
    return result, scales.reshape(each, high - low, cols_blocks)


def plan(sub_rows, labels):
    every = [("fsdp", i) for i in range(labels.parts_bits)]
    grp = [("grp", i) for i in range(labels.groups_bits)]
    unit = sub_rows // 16
    stages = [Stage("all", every), Stage("xor", grp)]
    spans = ((14, 1, 1), (0, 8, 4), (8, 4, 4), (12, 2, 2), (15, 1, 1))
    chunks = [(unit * first, unit * count, unit * at_once, stages) for first, count, at_once in spans]
    n = len(chunks)
    order = [0, 1]
    for c in range(n):
        order += [c]
        if c >= 1 and c < n - 1:
            order += [c - 1]
        if c + 2 < n:
            order += [c + 2]
    return chunks, order + [n - 2, n - 1]


def chunked_body(weight):
    rows_dev, cols_dev = weight.shape
    parts = lax.axis_size("fsdp")
    groups = lax.axis_size("grp")
    sub_rows = rows_dev // PALEY
    labels = Labels(parts, groups)
    chunks, order = plan(sub_rows, labels)
    state = {}
    result, scales, finished, token = None, [], [], ()
    for c in order:
        first, count, at_once, stages = chunks[c]
        if c not in state:
            arrays, names = make_pieces(
                weight, first, count, at_once, parts, token, stages[0], labels
            )
            token = (arrays[0],)
            state[c] = (0, stages[0].send(arrays), names)
            continue
        at, arrays, names = state[c]
        absolute = any(s.kind == "all" and s.bits[0][0] == "grp" for s in stages)
        if at + 1 < len(stages):
            arrays, names = mix_pieces(arrays, names, stages[at], stages[at + 1], labels, token, absolute)
            token = (arrays[0],)
            state[c] = (at + 1, stages[at + 1].send(arrays), names)
            continue
        low, high = first * PALEY, (first + count) * PALEY
        finished.append((low, high, arrays, names, stages[at]))
        ready = [
            b
            for b in range(low // BLOCK, -(-high // BLOCK))
            if sum(
                max(0, min(f[1], (b + 1) * BLOCK) - max(f[0], b * BLOCK)) for f in finished
            ) == BLOCK
        ]
        if ready:
            result, found = finish(
                result, finished, ready[0], ready[-1] + 1, rows_dev, groups, labels, token
            )
            token = (found,)
            scales.append((ready[0], found))
    scales = jnp.concatenate([found for _, found in sorted(scales, key=lambda s: s[0])], axis=1)
    return result, scales.reshape(-1, scales.shape[-1])


def body(weight):
    rows_dev, cols_dev = weight.shape
    parts = lax.axis_size("fsdp")
    groups = lax.axis_size("grp")
    tiled = (
        cols_dev % (parts * LANES) == 0
        and rows_dev % (8 * PALEY) == 0
        and rows_dev % BLOCK == 0
        and parts % groups == 0
        and parts <= 8
    )
    return chunked_body(weight) if tiled else plain_body(weight)


def solution(mesh):
    in_specs = (P("fsdp", "grp"),)
    out_specs = (P("grp", "fsdp"), P("grp", "fsdp"))
    return jax.shard_map(body, mesh=mesh, in_specs=in_specs, out_specs=out_specs, check_vma=False)
```

```python
import functools
import math

import jax
import jax.numpy as jnp
import numpy as np
from jax import lax
from jax.experimental import pallas as pl
from jax.experimental.pallas import tpu as pltpu
from jax.sharding import PartitionSpec as P

D = 8192
BLOCK = 128
FF = 26624
PALEY = 52
LANES = 128
SPLIT = 2


def paley_signs():
    squares_set = set()
    for coord_one in range(5):
        for coord_two in range(5):
            if coord_one or coord_two:
                squares_set.add(
                    (
                        (coord_one * coord_one + 2 * coord_two * coord_two) % 5,
                        2 * coord_one * coord_two % 5,
                    )
                )
    conference = np.zeros((26, 26), np.float32)
    conference[0, 1:] = 1.0
    conference[1:, 0] = 1.0
    for row_elem in range(25):
        for col_elem in range(25):
            diff_one = (row_elem % 5 - col_elem % 5) % 5
            diff_two = (row_elem // 5 - col_elem // 5) % 5
            if diff_one or diff_two:
                conference[1 + row_elem, 1 + col_elem] = (
                    1.0 if (diff_one, diff_two) in squares_set else -1.0
                )
    plus_block = np.array([[1.0, 1.0], [1.0, -1.0]], np.float32)
    minus_block = np.array([[1.0, -1.0], [-1.0, -1.0]], np.float32)
    return (
        np.kron(conference, plus_block) + np.kron(np.eye(26, dtype=np.float32), minus_block)
    ).astype(np.float32)


def sylvester(order):
    table = np.ones((1, 1), np.float32)
    while table.shape[0] < order:
        table = np.kron(np.array([[1.0, 1.0], [1.0, -1.0]], np.float32), table)
    return table


def sign_table(order, dtype):
    if order <= 64:
        indices = lax.iota(jnp.int32, order)
        parity = jnp.zeros((order, order), jnp.int32)
        for bit_pos in range(max(order.bit_length() - 1, 0)):
            parity = parity + (indices[:, None] >> bit_pos & 1) * (indices[None, :] >> bit_pos & 1)
        return (1 - 2 * (parity & 1)).astype(dtype)
    outer_part = sign_table(order // 64, dtype)
    inner_part = sign_table(64, dtype)
    return (outer_part[:, None, :, None] * inner_part[None, :, None, :]).reshape(order, order)


def plain_body(weight):
    exact_prec = lax.Precision.HIGHEST
    rows_dev, cols_dev = weight.shape
    parts = lax.axis_size("fsdp")
    groups = lax.axis_size("grp")
    sub_rows = rows_dev // 52
    piece = cols_dev // parts
    piece_signs = sign_table(piece, jnp.bfloat16)
    parts_signs = sign_table(parts, jnp.float32)
    paley = jnp.asarray(paley_signs(), jnp.float32)
    sub_signs = sign_table(sub_rows, jnp.float32)
    group_signs = sign_table(groups, jnp.float32)
    inner_done = jnp.einsum(
        "rab,bj->raj",
        weight.reshape(rows_dev, parts, piece),
        piece_signs,
        preferred_element_type=jnp.float32,
    )
    rotated = jnp.einsum("ap,raj->prj", parts_signs, inner_done, precision=exact_prec)
    rotated = rotated.reshape(parts, sub_rows, 52, piece)
    rotated = jnp.einsum("ab,pcbj->pcaj", paley, rotated, precision=exact_prec)
    rotated = jnp.einsum("ce,peaj->pcaj", sub_signs, rotated, precision=exact_prec)
    rotated = rotated.reshape(parts, sub_rows, 52 * piece)
    fsdp_signs = sign_table(parts, jnp.float32)
    mixed = jnp.einsum(
        "fg,gnx->fnx",
        fsdp_signs,
        lax.all_to_all(rotated, "fsdp", split_axis=0, concat_axis=0, tiled=True),
        precision=exact_prec,
    )
    count = mixed.shape[1]
    stacked = mixed.reshape(1, parts, count, 52 * piece)
    moved = lax.all_to_all(stacked, "grp", split_axis=1, concat_axis=0, tiled=True)
    moved = moved.reshape(groups, parts // groups, count, 52, piece)
    result = jnp.einsum("qg,gmnaj->mnaqj", group_signs, moved, precision=exact_prec)
    cols_out = groups * piece
    final = result.reshape(-1, cols_out) * (1.0 / math.sqrt(FF * D))
    rows_out = final.shape[0]
    blocks = final.reshape(rows_out // BLOCK, BLOCK, cols_out // BLOCK, BLOCK)
    scales = jnp.max(jnp.abs(blocks), axis=(1, 3))
    quantized = (
        (blocks / (scales[:, None, :, None] + 1e-06))
        .astype(jnp.bfloat16)
        .reshape(rows_out, cols_out)
    )
    return (quantized, scales)


def parity_sign(bits, order):
    parity = bits
    shift = 1
    while shift < order.bit_length():
        parity = parity ^ (parity >> shift)
        shift *= 2
    return 1.0 - 2.0 * (parity & 1).astype(jnp.float32)


def butterfly(values):
    values = list(values)
    half = 1
    while half < len(values):
        for low in range(len(values)):
            if not low & half:
                one, two = values[low], values[low + half]
                values[low], values[low + half] = one + two, one - two
        half *= 2
    return values


def compiler_params(limit):
    return pltpu.CompilerParams(vmem_limit_bytes=limit)


TINY = pl.CostEstimate(flops=0, bytes_accessed=0, transcendentals=0)
LONG = pl.CostEstimate(flops=10**12, bytes_accessed=4 * 10**9, transcendentals=0)
ANYWHERE = pl.BlockSpec(memory_space=pl.ANY)


class Labels:
    def __init__(self, parts, groups):
        self.parts_bits = parts.bit_length() - 1
        self.groups_bits = groups.bit_length() - 1
        self.slab_bits = self.parts_bits - self.groups_bits

    def start(self):
        return [("p", i) for i in range(self.parts_bits)]

    def split(self, axis, bit):
        return ("p" if axis == "fsdp" else "g", bit)

    def made(self, axis, bit):
        if axis == "grp":
            return ("k", bit)
        return ("m", bit) if bit < self.slab_bits else ("g", bit - self.slab_bits)


def slot_of(labels, values):
    return sum(values[label] << at for at, label in enumerate(labels))


def values_of(labels, slot):
    return {label: slot >> at & 1 for at, label in enumerate(labels)}


class Stage:
    def __init__(self, kind, bits):
        self.kind, self.bits = kind, bits
        self.fan = 1 << len(bits)

    def send(self, arrays):
        if self.kind == "all":
            return [lax.all_to_all(arrays[0], self.bits[0][0], split_axis=0, concat_axis=0, tiled=True)]
        if self.kind == "sum":
            axis, bit = self.bits[0]
            pairs = [[i, i ^ 1 << bit] for i in range(lax.axis_size(axis)) if not i >> bit & 1]
            both = lax.psum_scatter(
                arrays[0], axis, scatter_dimension=0, axis_index_groups=pairs, tiled=False
            )
            return [arrays[0], both]
        received = [arrays[0]]
        axes = {axis for axis, _ in self.bits}
        sizes = {axis: lax.axis_size(axis) for axis in axes}
        for e in range(1, self.fan):
            masks = {axis: 0 for axis in axes}
            for at, (axis, bit) in enumerate(self.bits):
                masks[axis] |= (e >> at & 1) << bit
            used = [axis for axis in ("fsdp", "grp") if masks.get(axis)]
            assert len(used) == 1
            axis = used[0]
            pairs = [(i, i ^ masks[axis]) for i in range(sizes[axis])]
            received.append(lax.ppermute(arrays[e], axis, pairs))
        return received

    def place(self):
        if self.kind == "all":
            return None
        place = 0
        for at, (axis, bit) in enumerate(self.bits):
            place = place | ((lax.axis_index(axis) >> bit) & 1) << at
        return place

    def arrived(self, refs, *index):
        if self.kind == "sum":
            axis, bit = self.bits[0]
            return [refs[0].at[(lax.axis_index(axis) >> bit & 1,) + index], refs[1].at[index]]
        return self.views(refs, self.fan, *index)

    def values(self, found):
        return [found[0], found[1] - found[0]] if self.kind == "sum" else found

    def views(self, refs, fan, *index):
        if self.kind != "xor":
            return [refs[0].at[(e,) + index] for e in range(fan)]
        return [refs[e].at[index] for e in range(fan)]

    def shapes(self, slots, rows, piece):
        if self.kind != "xor":
            return [jax.ShapeDtypeStruct((self.fan, slots, rows, piece), jnp.float32)]
        return [jax.ShapeDtypeStruct((slots, rows, piece), jnp.float32)] * self.fan

    def blocks(self, slots, rows, piece, arrived=False):
        where = lambda at, *inner: (0, at, 0)
        if self.kind != "xor":
            whole = pl.BlockSpec((self.fan, slots, rows, piece), lambda *at: (0,) + where(*at))
            after = [pl.BlockSpec((slots, rows, piece), where)] if self.kind == "sum" and arrived else []
            return [whole] + after
        return [pl.BlockSpec((slots, rows, piece), where)] * self.fan


def combine(stage, made, values, absolute=False):
    place, toward = stage.place(), None
    for at, label in enumerate(made):
        if label[0] == "g" and not absolute:
            bit = ((lax.axis_index("grp") >> label[1]) & 1) << at
            toward = bit if toward is None else toward | bit
    if toward is not None:
        values = [values[0]] + [
            parity_sign(toward & e, stage.fan) * values[e] for e in range(1, stage.fan)
        ]
    sums = butterfly(values)
    if place is not None:
        toward = 0 if toward is None else toward
        sums = [parity_sign((w ^ toward) & place, stage.fan) * sums[w] for w in range(stage.fan)]
    return sums


def make_pieces(weight, first, count, at_once, parts, after, stage, labels):
    rows_dev, cols_dev = weight.shape
    piece = cols_dev // parts
    sub_rows = rows_dev // PALEY
    rows = at_once * PALEY
    base = jnp.asarray(np.kron(sylvester(at_once), paley_signs()), jnp.bfloat16)
    inner = jnp.asarray(sylvester(piece), jnp.bfloat16)
    names = labels.start()
    cut = [labels.split(*bit) for bit in stage.bits]
    rest_names = [name for name in names if name not in cut]

    def halves(values):
        high = values.astype(jnp.bfloat16)
        return high, (values - high.astype(jnp.float32)).astype(jnp.bfloat16)

    def kernel(base_ref, inner_ref, *refs):
        w_refs, refs = refs[:SPLIT], refs[SPLIT:]
        outs, held, summed = refs[len(after):-2], refs[-2], refs[-1]
        turn, step = pl.program_id(0), pl.program_id(1)
        far_signs = [
            parity_sign((first + turn * at_once) & far, sub_rows)
            for far in range(0, sub_rows, at_once)
        ]
        me = None if stage.kind == "all" else lax.axis_index("fsdp")

        def gather(at, carry):
            here = pl.multiple_of(at * 16, 16)
            total = None
            for far, sign in enumerate(far_signs):
                part, inside = divmod(far * rows, rows_dev // SPLIT)
                term = w_refs[part][pl.ds(here + inside, 16), :].astype(jnp.float32)
                total = term if total is None else total + sign * term
            summed[pl.ds(here, 16), :] = total
            return carry

        lax.fori_loop(0, rows // 16, gather, 0)
        high, low = halves(summed[...])
        turned = jnp.dot(base_ref[...], high, preferred_element_type=jnp.float32) + jnp.dot(
            base_ref[...], low, preferred_element_type=jnp.float32
        )
        high, low = halves(turned)
        turned = jnp.dot(high, inner_ref[...], preferred_element_type=jnp.float32) + jnp.dot(
            low, inner_ref[...], preferred_element_type=jnp.float32
        )
        held[step] = turned

        @pl.when(step == parts - 1)
        def _():
            before = [1.0 if me is None else parity_sign(a & me, parts) for a in range(parts)]

            def body(at, carry):
                here = pl.ds(pl.multiple_of(at * 16, 16), 16)
                values = [held[a, here, :] for a in range(parts)]
                if me is not None:
                    values = [values[0]] + [before[a] * values[a] for a in range(1, parts)]
                for j, value in enumerate(butterfly(values)):
                    digits = values_of(names, j)
                    targets = stage.views(outs, stage.fan, slot_of(rest_names, digits), here)
                    targets[slot_of(cut, digits)][...] = value
                return carry

            lax.fori_loop(0, rows // 16, body, 0)

    whole = lambda turn, step: (0, 0)
    slots = 1 << len(rest_names)
    return pl.pallas_call(
        kernel,
        grid=(count // at_once, parts),
        in_specs=[
            pl.BlockSpec((rows, rows), whole, pipeline_mode=pl.Buffered(1)),
            pl.BlockSpec((piece, piece), whole, pipeline_mode=pl.Buffered(1)),
        ]
        + [
            pl.BlockSpec((rows_dev // SPLIT, piece), functools.partial(lambda part, turn, step: (part, step), part))
            for part in range(SPLIT)
        ]
        + [ANYWHERE] * len(after),
        out_specs=stage.blocks(slots, rows, piece),
        out_shape=stage.shapes(slots, count * PALEY, piece),
        scratch_shapes=[
            pltpu.VMEM((parts, rows, piece), jnp.float32),
            pltpu.VMEM((rows, piece), jnp.float32),
        ],
        compiler_params=compiler_params(48 * 2**20),
        cost_estimate=TINY,
        name="make_pieces",
    )(base, inner, *[weight] * SPLIT, *after), rest_names


def mix_pieces(arrays, names, came, going, labels, after, absolute):
    rows, piece = arrays[0].shape[-2:]
    made = [labels.made(*bit) for bit in came.bits]
    cut = [labels.split(*bit) for bit in going.bits]
    rest_names = [name for name in names + made if name not in cut]
    slots_in, slots_out = 1 << len(names), 1 << len(rest_names)
    strip, tile = 16, rows
    for size in (104, 208):
        if rows % size == 0:
            tile = size

    def kernel(*refs):
        ins, outs = refs[: len(arrays)], refs[len(arrays) + len(after):]

        def body(at, carry):
            here = pl.ds(pl.multiple_of(at * strip, strip), strip)
            for slot in range(slots_in):
                values = came.values([view[...] for view in came.arrived(ins, slot, here)])
                for w, value in enumerate(combine(came, made, values, absolute)):
                    digits = {**values_of(names, slot), **values_of(made, w)}
                    target = going.views(outs, going.fan, slot_of(rest_names, digits), here)
                    if going.kind == "sum":
                        index = slot_of(cut, digits) ^ going.place()
                        outs[0][index, slot_of(rest_names, digits), here, :] = value
                    else:
                        target[slot_of(cut, digits)][...] = value
            return carry

        lax.fori_loop(0, tile // strip, body, 0)

    return pl.pallas_call(
        kernel,
        grid=(rows // tile,),
        in_specs=came.blocks(slots_in, tile, piece, True) + [ANYWHERE] * len(after),
        out_specs=going.blocks(slots_out, tile, piece),
        out_shape=going.shapes(slots_out, rows, piece),
        compiler_params=compiler_params(24 * 2**20),
        cost_estimate=TINY,
        name="mix_pieces",
    )(*arrays, *after), rest_names


def finish(target, chunks, low, high, rows_slab, groups, labels, after):
    piece = chunks[0][2][0].shape[-1]
    each = 1 << labels.slab_bits
    cols_out = groups * piece
    cols_blocks = cols_out // BLOCK
    blocks = [(m, b) for m in range(each) for b in range(low, high)]
    needed = [c for c in chunks if c[0] < high * BLOCK and c[1] > low * BLOCK]
    for c in needed:
        assert c[3] == needed[0][3] and c[4].bits == needed[0][4].bits
        assert c[4].kind == needed[0][4].kind
    names, came = needed[0][3], needed[0][4]
    made = [labels.made(*bit) for bit in came.bits]
    factor = 1.0 / math.sqrt(FF * D)
    operands = [array for c in needed for array in c[2]]
    starts = np.cumsum([0] + [len(c[2]) for c in needed])
    aliased = target is not None
    per_block = {
        b: [
            (at, max(c[0], b * BLOCK), min(c[1], (b + 1) * BLOCK))
            for at, c in enumerate(needed)
            if max(c[0], b * BLOCK) < min(c[1], (b + 1) * BLOCK)
        ]
        for b in range(low, high)
    }
    most = max(len(s) for s in per_block.values())
    slab_names = [name for name in names if name[0] == "m"]
    column_names = [name for name in names if name[0] == "k"]
    column_slots = 1 << len(column_names)

    def kernel(*refs):
        ins = refs[: len(operands)]
        out, scales_ref, held, ready, in_sems, out_sems = refs[
            len(operands) + int(aliased) + len(after):
        ]
        reads = []
        for at, (m, b) in enumerate(blocks):
            copies = []
            for seg, (c, start, stop) in enumerate(per_block[b]):
                base, sources = needed[c][0], ins[starts[c] : starts[c + 1]]
                for column in range(column_slots):
                    digits = {**values_of(slab_names, m), **values_of(column_names, column)}
                    views = came.arrived(
                        sources, slot_of(names, digits), pl.ds(start - base, stop - start)
                    )
                    for e, view in enumerate(views):
                        copy = pltpu.make_async_copy(
                            view,
                            held.at[at, column, e, pl.ds(start - b * BLOCK, stop - start), :],
                            in_sems.at[at, column, e, seg],
                        )
                        copy.start()
                        copies.append(copy)
            reads.append(copies)
        lane = lax.broadcasted_iota(jnp.int32, (1, cols_blocks), 1)
        writes = []
        for at, (m, b) in enumerate(blocks):
            for copy in reads[at]:
                copy.wait()
            found = jnp.zeros((1, cols_blocks), jnp.float32)
            for part in range(piece // BLOCK):
                span = pl.ds(part * BLOCK, BLOCK)
                for column in range(column_slots):
                    values = came.values([held[at, column, e, :, span] for e in range(came.fan)])
                    values = [value * factor for value in values]
                    for w, value in enumerate(combine(came, made, values)):
                        digits = {**values_of(column_names, column), **values_of(made, w)}
                        group = sum(bit << name[1] for name, bit in digits.items())
                        top = jnp.max(
                            jnp.max(jnp.abs(value), axis=0, keepdims=True), axis=1, keepdims=True
                        )
                        place = group * (piece // BLOCK) + part
                        found = jnp.where(lane == place, top, found)
                        ready[at, :, pl.ds(place * BLOCK, BLOCK)] = (
                            value * (1.0 / (top + 1e-06))
                        ).astype(jnp.bfloat16)
            scales_ref[pl.ds(at, 1), :] = found
            copy = pltpu.make_async_copy(
                ready.at[at],
                out.at[pl.ds(m * rows_slab + b * BLOCK, BLOCK), :],
                out_sems.at[at],
            )
            copy.start()
            writes.append(copy)
        for copy in writes:
            copy.wait()

    total = len(blocks)
    result, scales = pl.pallas_call(
        kernel,
        in_specs=[ANYWHERE] * (len(operands) + int(aliased) + len(after)),
        out_specs=[ANYWHERE, pl.BlockSpec(memory_space=pltpu.VMEM)],
        out_shape=[
            jax.ShapeDtypeStruct((each * rows_slab, cols_out), jnp.bfloat16),
            jax.ShapeDtypeStruct((total, cols_blocks), jnp.float32),
        ],
        scratch_shapes=[
            pltpu.VMEM((total, column_slots, came.fan, BLOCK, piece), jnp.float32),
            pltpu.VMEM((total, BLOCK, cols_out), jnp.bfloat16),
            pltpu.SemaphoreType.DMA((total, column_slots, came.fan, most)),
            pltpu.SemaphoreType.DMA((total,)),
        ],
        input_output_aliases={len(operands): 0} if aliased else {},
        compiler_params=compiler_params(28 * 2**20),
        cost_estimate=LONG,
        name="finish",
    )(*operands, *([target] if aliased else []), *after)
    return result, scales.reshape(each, high - low, cols_blocks)


def plan(sub_rows, labels):
    every = [("fsdp", i) for i in range(labels.parts_bits)]
    grp = [("grp", i) for i in range(labels.groups_bits)]
    unit = sub_rows // 16
    stages = [Stage("all", every), Stage("xor", grp)]
    spans = ((14, 1, 1), (0, 8, 4), (8, 4, 4), (12, 2, 2), (15, 1, 1))
    chunks = [(unit * first, unit * count, unit * at_once, stages) for first, count, at_once in spans]
    n = len(chunks)
    order = [0, 1]
    for c in range(n):
        order += [c]
        if c >= 1 and c < n - 1:
            order += [c - 1]
        if c + 2 < n:
            order += [c + 2]
    return chunks, order + [n - 2, n - 1]


def chunked_body(weight):
    rows_dev, cols_dev = weight.shape
    parts = lax.axis_size("fsdp")
    groups = lax.axis_size("grp")
    sub_rows = rows_dev // PALEY
    labels = Labels(parts, groups)
    chunks, order = plan(sub_rows, labels)
    state = {}
    result, scales, finished, token = None, [], [], ()
    for c in order:
        first, count, at_once, stages = chunks[c]
        if c not in state:
            arrays, names = make_pieces(
                weight, first, count, at_once, parts, token, stages[0], labels
            )
            token = (arrays[0],)
            state[c] = (0, stages[0].send(arrays), names)
            continue
        at, arrays, names = state[c]
        absolute = any(s.kind == "all" and s.bits[0][0] == "grp" for s in stages)
        if at + 1 < len(stages):
            arrays, names = mix_pieces(arrays, names, stages[at], stages[at + 1], labels, token, absolute)
            token = (arrays[0],)
            state[c] = (at + 1, stages[at + 1].send(arrays), names)
            continue
        low, high = first * PALEY, (first + count) * PALEY
        finished.append((low, high, arrays, names, stages[at]))
        ready = [
            b
            for b in range(low // BLOCK, -(-high // BLOCK))
            if sum(
                max(0, min(f[1], (b + 1) * BLOCK) - max(f[0], b * BLOCK)) for f in finished
            ) == BLOCK
        ]
        if ready:
            result, found = finish(
                result, finished, ready[0], ready[-1] + 1, rows_dev, groups, labels, token
            )
            token = (found,)
            scales.append((ready[0], found))
    scales = jnp.concatenate([found for _, found in sorted(scales, key=lambda s: s[0])], axis=1)
    return result, scales.reshape(-1, scales.shape[-1])


def body(weight):
    rows_dev, cols_dev = weight.shape
    parts = lax.axis_size("fsdp")
    groups = lax.axis_size("grp")
    tiled = (
        cols_dev % (parts * LANES) == 0
        and rows_dev % (8 * PALEY) == 0
        and rows_dev % BLOCK == 0
        and parts % groups == 0
        and parts <= 8
    )
    return chunked_body(weight) if tiled else plain_body(weight)


def solution(mesh):
    in_specs = (P("fsdp", "grp"),)
    out_specs = (P("grp", "fsdp"), P("grp", "fsdp"))
    return jax.shard_map(body, mesh=mesh, in_specs=in_specs, out_specs=out_specs, check_vma=False)
```
